32 devices in a mesh: expert: 8 (over z, y), tensor: 4 (over x, core).
Axes of the slice: x: 2, y: 2, z: 4, core: 2. Of those that a mesh axis runs over, the one named last changes fastest.
Arguments:
- tokens: bfloat16 [1024, 2048], P('expert', 'tensor'), may hold values from -6 to 6
- labels: int32 [1024, 1], P('expert'), may hold values from 0 to 3, as said below
- domain_ids: int32 [1024], P('expert'), may hold values from 0 to 21
- domain_weights: float32 [22], replicated, may hold values from 0.02 to 0.5
- cotangent: bfloat16 [1024, 2048], P('expert', 'tensor'), may hold values from -6 to 6
- gate_weight: bfloat16 [8, 2048, 2048], P('expert', None, 'tensor'), may hold values from -0.125 to 0.125
- up_weight: bfloat16 [8, 2048, 2048], P('expert', None, 'tensor'), may hold values from -0.125 to 0.125
- down_weight: bfloat16 [8, 2048, 2048], P('expert', 'tensor'), may hold values from -0.09375 to 0.09375
Outputs:
- layer_out: bfloat16 [1024, 2048], P('expert', 'tensor')
- input_grad: bfloat16 [1024, 2048], P('expert', 'tensor')
- gate_grad: bfloat16 [8, 2048, 2048], P('expert', None, 'tensor')
- up_grad: bfloat16 [8, 2048, 2048], P('expert', None, 'tensor')
- down_grad: bfloat16 [8, 2048, 2048], P('expert', 'tensor')
The draws below stay inside these ranges and needn't reach their ends.
Inputs may be any that keep to these rules, and one draw needn't show every extreme that they name: `labels`: among the rows of one device (aligned blocks of 128 rows) no label appears more than 64 times, and every such block has some label exactly 64 times.
All inputs are finite; a program needn't handle non-finite values.
Results may differ from the reference program's by a relative error of at most 0.0058.
Values may be sent and summed in bfloat16 or wider, within the bound.
A program may use at most 320 MiB of HBM per device.

```python
import math
import jax
import jax.numpy as jnp
from jax import lax

D = 2048
FF = 4096
SPLIT = 2
NDOM = 22
TOK_DEV = 128
EXPERTS = 4
CAP = 64
TOKENS = 1024


def label_block(block_key):
    key_full, key_pick, key_order = jax.random.split(block_key, 3)
    total_slots = EXPERTS * CAP
    slot_ids = jnp.arange(total_slots, dtype=jnp.int32)
    slot_owner = slot_ids // CAP
    forced = jax.random.randint(key_full, (), 0, EXPERTS, dtype=jnp.int32)
    shuffled = jax.random.permutation(key_pick, slot_ids).astype(jnp.int32)
    priority = shuffled + jnp.where(slot_owner == forced, -total_slots, 0).astype(jnp.int32)
    picked = jnp.argsort(priority, stable=True)[:TOK_DEV].astype(jnp.int32)
    block_labels = picked // CAP
    order = jax.random.permutation(key_order, jnp.arange(TOK_DEV, dtype=jnp.int32))
    return block_labels[order].astype(jnp.int32)


def draw_labels(key, part):
    blocks = TOKENS // TOK_DEV
    block_keys = jax.random.split(jax.random.fold_in(key, 7), blocks)
    labels_all = jax.vmap(label_block)(block_keys)
    return labels_all.reshape(TOKENS, 1).astype(jnp.int32)


def touch_ends(values, own_key, low, top_value):
    index_at = [jax.random.randint(jax.random.fold_in(own_key, axis), (), 0, length) for axis, length in enumerate(values.shape)]
    main_axis = values.shape.index(max(values.shape))
    neighbour = index_at[:main_axis] + [(index_at[main_axis] + 1) % values.shape[main_axis]] + index_at[main_axis + 1:]
    return values.at[tuple(index_at)].set(low).at[tuple(neighbour)].set(top_value)


def block_levels(stream_key, extent, shards, smallest, top_value):
    level = 1.0
    for axis_at, blocks in shards:
        steps = jax.random.uniform(jax.random.fold_in(jax.random.fold_in(stream_key, 6), axis_at), (blocks,), jnp.float32, smallest / len(shards), top_value / len(shards))
        level = level * jnp.repeat(jnp.exp(steps), extent[axis_at] // blocks).reshape((-1,) + (1,) * (len(extent) - 1 - axis_at))
    return level


def centred(rng, shape, width, reach, cuts=(), kind=jnp.bfloat16):
    loudness = block_levels(rng, shape, cuts, -0.22, 0.18) if cuts else 1.0
    entries = jax.random.normal(rng, shape, jnp.float32) * width * loudness
    return jnp.minimum(jnp.maximum(entries, -reach), reach).astype(kind)


def setup_inputs(seed: int = 0) -> dict:
    arg_keys = jax.random.split(jax.random.key(seed), 9)
    return {
        "tokens": centred(arg_keys[0], (TOKENS, D), 1.0, 6.0, ((0, 8), (1, 4))),
        "labels": draw_labels(jax.random.fold_in(arg_keys[8], 71), 0),
        "domain_ids": touch_ends(jax.random.randint(arg_keys[2], (TOKENS,), 0, NDOM), jax.random.fold_in(arg_keys[2], 1), 0, NDOM - 1).astype(jnp.int32),
        "domain_weights": jnp.clip(jnp.exp(jax.random.uniform(arg_keys[3], (NDOM,), jnp.float32, math.log(0.02), math.log(0.5))), 0.02, 0.5),
        "cotangent": centred(arg_keys[4], (TOKENS, D), 1.0, 6.0, ((0, 8), (1, 4))),
        "gate_weight": centred(arg_keys[5], (EXPERTS * SPLIT, D, FF // SPLIT), D ** -0.5, 0.125, ((0, 8), (2, 4))),
        "up_weight": centred(arg_keys[6], (EXPERTS * SPLIT, D, FF // SPLIT), D ** -0.5, 0.125, ((0, 8), (2, 4))),
        "down_weight": centred(arg_keys[7], (EXPERTS * SPLIT, FF // SPLIT, D), FF ** -0.5, 0.09375, ((0, 8), (1, 4))),
    }


def silu_parts(gate_pre):
    squash = jax.nn.sigmoid(gate_pre)
    return squash, gate_pre * squash


def reference(tokens, labels, domain_ids, domain_weights, cotangent, gate_weight, up_weight, down_weight):
    lang_label = labels[:, 0]
    grad_rows = (domain_weights[domain_ids][:, None] * cotangent.astype(jnp.float32)).astype(jnp.bfloat16)
    blocks = TOKENS // TOK_DEV
    grouped = lang_label.reshape(blocks, TOK_DEV)
    positions = jnp.arange(TOK_DEV, dtype=jnp.int32)
    earlier = positions[None, :] < positions[:, None]
    same_label = grouped[:, :, None] == grouped[:, None, :]
    slot_pos = jnp.sum((same_label & earlier[None]).astype(jnp.int32), axis=2)
    position = (jnp.arange(blocks, dtype=jnp.int32)[:, None] * CAP + slot_pos).reshape(TOKENS).astype(jnp.int32)
    spill_row = blocks * CAP
    gate_all = gate_weight.reshape(EXPERTS, SPLIT, D, FF // SPLIT).transpose(0, 2, 1, 3).reshape(EXPERTS, D, FF)
    up_all = up_weight.reshape(EXPERTS, SPLIT, D, FF // SPLIT).transpose(0, 2, 1, 3).reshape(EXPERTS, D, FF)
    down_all = down_weight.reshape(EXPERTS, FF, D)

    def expert_step(running, pieces):
        out_sum, input_sum = running
        expert, w_gate, w_up, w_down = pieces
        chosen = lang_label == expert
        scatter_index = jnp.where(chosen, position, spill_row).astype(jnp.int32)
        routed = jnp.zeros((spill_row, D), jnp.bfloat16).at[scatter_index].set(tokens, mode="drop")
        routed_grad = jnp.zeros((spill_row, D), jnp.bfloat16).at[scatter_index].set(grad_rows, mode="drop")
        gate_pre = jnp.dot(routed, w_gate, preferred_element_type=jnp.float32)
        up_pre = jnp.dot(routed, w_up, preferred_element_type=jnp.float32)
        squash, activated = silu_parts(gate_pre)
        hidden = (activated * up_pre).astype(jnp.bfloat16)
        out_rows = jnp.dot(hidden, w_down, preferred_element_type=jnp.float32)
        grad_hidden = jnp.dot(routed_grad, w_down.T, preferred_element_type=jnp.float32)
        grad_gate_pre = (grad_hidden * up_pre * squash * (1.0 + gate_pre * (1.0 - squash))).astype(jnp.bfloat16)
        grad_up_pre = (grad_hidden * activated).astype(jnp.bfloat16)
        gate_part = jnp.dot(routed.T, grad_gate_pre, preferred_element_type=jnp.float32).astype(jnp.bfloat16)
        up_part = jnp.dot(routed.T, grad_up_pre, preferred_element_type=jnp.float32).astype(jnp.bfloat16)
        down_part = jnp.dot(hidden.T, routed_grad, preferred_element_type=jnp.float32).astype(jnp.bfloat16)
        input_rows = jnp.dot(grad_gate_pre, w_gate.T, preferred_element_type=jnp.float32) + jnp.dot(grad_up_pre, w_up.T, preferred_element_type=jnp.float32)
        zero_val = jnp.zeros((), jnp.float32)
        out_sum = out_sum + jnp.where(chosen[:, None], out_rows[position], zero_val)
        input_sum = input_sum + jnp.where(chosen[:, None], input_rows[position], zero_val)
        return (out_sum, input_sum), (gate_part, up_part, down_part)

    start = (jnp.zeros((TOKENS, D), jnp.float32), jnp.zeros((TOKENS, D), jnp.float32))
    xs_all = (jnp.arange(EXPERTS, dtype=jnp.int32), gate_all, up_all, down_all)
    (out_sum, input_sum), (gate_parts, up_parts, down_parts) = lax.scan(expert_step, start, xs_all)
    gate_grad = gate_parts.reshape(EXPERTS, D, SPLIT, FF // SPLIT).transpose(0, 2, 1, 3).reshape(EXPERTS * SPLIT, D, FF // SPLIT)
    up_grad = up_parts.reshape(EXPERTS, D, SPLIT, FF // SPLIT).transpose(0, 2, 1, 3).reshape(EXPERTS * SPLIT, D, FF // SPLIT)
    down_grad = down_parts.reshape(EXPERTS * SPLIT, FF // SPLIT, D)
    return (out_sum.astype(jnp.bfloat16), input_sum.astype(jnp.bfloat16), gate_grad, up_grad, down_grad)
```

```python
import jax
import jax.numpy as jnp
from jax import lax
from jax.experimental import pallas as pl
from jax.experimental.pallas import tpu as pltpu
from jax.sharding import PartitionSpec as P

SPLIT = 2
F32 = jnp.float32
BF16 = jnp.bfloat16
MESH = pl.DeviceIdType.MESH
(
    ZOUT, XOWN, YOWN, SOWN, FWDA, FWDB, SPX, SPY, SPD,
    RSIB, RDA, RDB, RX, RY, RZ, KINDS,
) = range(16)


def partner(value, axis, stride):
    return lax.ppermute(value, axis, [(i, i ^ 1 << stride) for i in range(lax.axis_size(axis))])


def silu_parts(gate_pre):
    squash = jax.nn.sigmoid(gate_pre)
    return (squash, gate_pre * squash)


def body(
    tokens, labels, domain_ids, domain_weights, cotangent, gate_weight, up_weight, down_weight
):
    n_expert = lax.axis_size("expert")
    tok_rows = tokens.shape[0]
    experts_all = n_expert // SPLIT
    capacity = 2 * tok_rows // experts_all
    half_cap = capacity // 2
    parity = lax.axis_index("expert") % 2
    lang_label = labels[:, 0]
    dom_hot = (
        domain_ids[:, None] == jnp.arange(domain_weights.shape[0], dtype=jnp.int32)[None, :]
    ).astype(jnp.float32)
    tok_scale = jnp.sum(dom_hot * domain_weights[None, :], axis=1)
    grad_rows = (tok_scale[:, None] * cotangent.astype(jnp.float32)).astype(jnp.bfloat16)
    lab_hot = (lang_label[:, None] == jnp.arange(experts_all, dtype=jnp.int32)[None, :]).astype(
        jnp.float32
    )
    row_ids = jnp.arange(tok_rows, dtype=jnp.int32)
    earlier = (row_ids[None, :] < row_ids[:, None]).astype(jnp.float32)
    before = jnp.dot(earlier, lab_hot, precision=lax.Precision.HIGHEST)
    slot_pos = jnp.sum(before * lab_hot, axis=1).astype(jnp.int32)
    target_row = lang_label * capacity + slot_pos
    sources = jnp.stack((tokens, grad_rows))
    sources = lax.all_gather(sources, "tensor", axis=2, tiled=True)
    slot_ids = jnp.arange(n_expert * capacity, dtype=jnp.int32)
    dispatch_map = (slot_ids[:, None] // capacity // SPLIT == lang_label[None, :]) & (
        slot_ids[:, None] % capacity == slot_pos[None, :]
    )
    dispatch_map = dispatch_map.astype(jnp.bfloat16)
    outbound = jnp.einsum(
        "rt,ktw->krw", dispatch_map, sources, preferred_element_type=jnp.float32
    ).astype(jnp.bfloat16)
    outbound = outbound.reshape(2, n_expert, capacity, sources.shape[2])
    arrived = lax.all_to_all(outbound, "expert", split_axis=1, concat_axis=1, tiled=True)
    rows_all = n_expert * capacity
    feat_width = arrived.shape[3]
    routed = arrived[0].reshape(rows_all, feat_width)
    routed_grad = arrived[1].reshape(rows_all, feat_width)
    w_gate = gate_weight[0]
    w_up = up_weight[0]
    w_down = down_weight[0]
    contract_rows = (((0,), (0,)), ((), ()))
    contract_cols = (((1,), (1,)), ((), ()))
    gate_pre = jnp.dot(routed, w_gate, preferred_element_type=jnp.float32)
    up_pre = jnp.dot(routed, w_up, preferred_element_type=jnp.float32)
    squash, activated = silu_parts(gate_pre)
    hidden = (activated * up_pre).astype(jnp.bfloat16)
    out_part = jnp.dot(hidden, w_down, preferred_element_type=jnp.float32)
    grad_hidden = lax.dot_general(
        routed_grad, w_down, contract_cols, preferred_element_type=jnp.float32
    )
    grad_gate_pre = (grad_hidden * up_pre * squash * (1.0 + gate_pre * (1.0 - squash))).astype(
        jnp.bfloat16
    )
    grad_up_pre = (grad_hidden * activated).astype(jnp.bfloat16)
    gate_grad = lax.dot_general(
        routed, grad_gate_pre, contract_rows, preferred_element_type=jnp.float32
    ).astype(jnp.bfloat16)[None]
    up_grad = lax.dot_general(
        routed, grad_up_pre, contract_rows, preferred_element_type=jnp.float32
    ).astype(jnp.bfloat16)[None]
    down_grad = lax.dot_general(
        hidden, routed_grad, contract_rows, preferred_element_type=jnp.float32
    ).astype(jnp.bfloat16)[None]
    input_part = lax.dot_general(
        grad_gate_pre, w_gate, contract_cols, preferred_element_type=jnp.float32
    ) + lax.dot_general(grad_up_pre, w_up, contract_cols, preferred_element_type=jnp.float32)
    out_part = out_part.reshape(n_expert, capacity, feat_width)
    input_part = input_part.reshape(n_expert, capacity, feat_width)
    out_share, input_share = (
        lax.psum_scatter(out_part, "tensor", scatter_dimension=2, tiled=True),
        lax.psum_scatter(input_part, "tensor", scatter_dimension=2, tiled=True),
    )
    partial_value = jnp.stack((out_share, input_share))
    kept = jnp.where(parity == 0, partial_value[:, :, :half_cap], partial_value[:, :, half_cap:])
    handed = jnp.where(parity == 0, partial_value[:, :, half_cap:], partial_value[:, :, :half_cap])
    summed = kept + partner(handed, "expert", 0)
    going_back = summed.astype(jnp.bfloat16)
    returned = lax.all_to_all(going_back, "expert", split_axis=1, concat_axis=1, tiled=True)
    home_ids = jnp.arange(n_expert * half_cap, dtype=jnp.int32)
    home_map = (home_ids[:, None] == target_row[None, :]).astype(jnp.bfloat16)
    flat_back = returned.reshape(2, n_expert * half_cap, returned.shape[3])
    gathered_home = jnp.einsum(
        "rt,krw->ktw", home_map, flat_back, preferred_element_type=jnp.float32
    ).astype(jnp.bfloat16)
    return (gathered_home[0], gathered_home[1], gate_grad, up_grad, down_grad)


def expert_kernel(
    tok_ref, cot_ref, lab_ref, dom_ref, dw_ref, wg_hbm, wu_hbm, wd_hbm,
    y_ref, yg_ref, rows_hbm, hid_hbm, ggp_hbm, gup_hbm,
    wg, wu, wd, slots, rows, gate_pre, up_pre, hidden, ggp, gup, keep,
    sib_src, sib_dst, diag_src, diag_dst, nx_src, nx_dst, ny_src, ny_dst,
    back_src, back, send_sem, recv_sem, local_sem,
):
    n_tok, width = tok_ref.shape
    n_lang = slots.shape[0]
    cap = slots.shape[2]
    half = cap // 2
    block = 2 * cap
    ei = lax.axis_index("expert")
    ti = lax.axis_index("tensor")
    z, y = ei // 2, ei % 2
    x, c = ti // 2, ti % 2
    nx, ny = 1 - x, 1 - y
    tix = nx * 2 + c
    tis = x * 2 + 1 - c
    tixs = nx * 2 + 1 - c
    plane = [z, z + 1 - 2 * (z % 2), (z + 2) % 4, 3 - z]
    x_dev, y_dev, s_dev = (ei, tix), (z * 2 + ny, ti), (ei, tis)
    z_dev = [(plane[j] * 2 + y, ti) for j in range(n_lang)]

    loads = [
        pltpu.make_async_copy(wg_hbm.at[0], wg, local_sem.at[0]),
        pltpu.make_async_copy(wu_hbm.at[0], wu, local_sem.at[1]),
        pltpu.make_async_copy(wd_hbm.at[0], wd, local_sem.at[2]),
    ]
    barrier = pltpu.get_barrier_semaphore()
    others = [x_dev, y_dev, s_dev] + z_dev[1:]
    for dev in others:
        pl.semaphore_signal(barrier, inc=1, device_id=dev, device_id_type=MESH)
    for copy in loads:
        copy.start()

    lab = lab_ref[...]
    lane = lax.broadcasted_iota(jnp.int32, (n_tok, n_tok), 1)
    sub = lax.broadcasted_iota(jnp.int32, (n_tok, n_tok), 0)
    lab_hot = jnp.where(lane == lab, 1.0, 0.0)
    earlier = jnp.where(lane < sub, 1.0, 0.0).astype(BF16)
    before = jnp.dot(earlier, lab_hot.astype(BF16), preferred_element_type=F32)
    pos = jnp.sum(before * lab_hot, axis=1, keepdims=True)
    target = lab.astype(F32) * cap + pos
    slot_lane = lax.broadcasted_iota(jnp.int32, (n_tok, n_lang * cap), 1).astype(F32)
    to_slot = jnp.where(slot_lane == target, 1.0, 0.0).astype(BF16)
    dom_row = jnp.broadcast_to(dom_ref[...].astype(F32), (n_tok, n_tok))
    dom_col = jnp.sum(jnp.where(lane == sub, dom_row, 0.0), axis=1, keepdims=True)
    n_dom = dw_ref.shape[1]
    dom_lane = lax.broadcasted_iota(jnp.int32, (n_tok, n_dom), 1).astype(F32)
    dw_row = jnp.broadcast_to(dw_ref[...], (n_tok, n_dom))
    scale = jnp.sum(jnp.where(dom_lane == dom_col, dw_row, 0.0), axis=1, keepdims=True)
    grad_rows = (scale * cot_ref[...].astype(F32)).astype(BF16)
    over_tokens = (((0,), (0,)), ((), ()))
    for k, source in enumerate((tok_ref[...], grad_rows)):
        packed = lax.dot_general(
            to_slot, source, over_tokens, preferred_element_type=F32
        ).astype(BF16)
        for e in range(n_lang):
            slots[e, k] = packed[e * cap:(e + 1) * cap]

    started = []

    def copy(kind, k, j, src, dst, dev):
        return pltpu.make_async_remote_copy(
            src_ref=src, dst_ref=dst, send_sem=send_sem.at[kind, k, j],
            recv_sem=recv_sem.at[kind, k, j], device_id=dev, device_id_type=MESH,
        )

    def send(kind, k, j, src, dst, dev):
        going = copy(kind, k, j, src, dst, dev)
        going.start()
        started.append(going)

    def recv(kind, k, j, dst, dev):
        copy(kind, k, j, dst, dst, dev).wait_recv()

    def piece(k, f, j, row_y, part=None):
        first = j * block + row_y * cap
        size = cap
        if part is not None:
            first = first + part * half
            size = half
        return rows.at[k, f, pl.ds(pl.multiple_of(first, half), size)]

    pl.semaphore_wait(barrier, len(others))
    for k in range(2):
        for j in range(1, n_lang):
            send(ZOUT, k, j, slots.at[plane[j], k], piece(k, ti, j, y), z_dev[j])
    for k in range(2):
        piece(k, ti, 0, y)[...] = slots[z, k]

    def g0(q):
        k, j = q // n_lang, q % n_lang
        own = piece(k, ti, j, y)
        if j:
            recv(ZOUT, k, j, own, z_dev[j])
        send(XOWN, k, j, own, own, x_dev)
        send(YOWN, k, j, own, own, y_dev)
        send(SOWN, k, j, own, own, s_dev)

    def g1(q):
        k, j = q // n_lang, q % n_lang
        from_x, from_y = piece(k, tix, j, y), piece(k, ti, j, ny)
        recv(XOWN, k, j, from_x, x_dev)
        part = piece(k, tix, j, y, 0)
        send(FWDA, k, j, part, part, y_dev)
        send(SPX, k, j, from_x, from_x, s_dev)
        recv(YOWN, k, j, from_y, y_dev)
        part = piece(k, ti, j, ny, 1)
        send(FWDB, k, j, part, part, x_dev)
        send(SPY, k, j, from_y, from_y, s_dev)

    def g2(q):
        k, j = q // n_lang, q % n_lang
        recv(FWDA, k, j, piece(k, tix, j, ny, 0), y_dev)
        recv(FWDB, k, j, piece(k, tix, j, ny, 1), x_dev)
        diag = piece(k, tix, j, ny)
        send(SPD, k, j, diag, diag, s_dev)

    def g3(q):
        k, j = q // n_lang, q % n_lang
        recv(SOWN, k, j, piece(k, tis, j, y), s_dev)
        recv(SPX, k, j, piece(k, tixs, j, y), s_dev)
        recv(SPY, k, j, piece(k, tis, j, ny), s_dev)
        recv(SPD, k, j, piece(k, tixs, j, ny), s_dev)

    size = 2 * block
    n_feat = rows.shape[1]
    over_cols = (((1,), (1,)), ((), ()))

    def all_feats(k, g):
        return jnp.concatenate(
            [rows[k, f, g * size:(g + 1) * size] for f in range(n_feat)], axis=1
        )

    def forward(g):
        at = slice(g * size, (g + 1) * size)
        here = all_feats(0, g)
        gp = jnp.dot(here, wg[...], preferred_element_type=F32)
        up = jnp.dot(here, wu[...], preferred_element_type=F32)
        gate_pre[at] = gp
        up_pre[at] = up
        hidden[at] = (gp * jax.nn.sigmoid(gp) * up).astype(BF16)

    def backward(g):
        at = slice(g * size, (g + 1) * size)
        gh = lax.dot_general(all_feats(1, g), wd[...], over_cols, preferred_element_type=F32)
        gp, up = gate_pre[at], up_pre[at]
        s = jax.nn.sigmoid(gp)
        ggp[at] = (gh * up * s * (1.0 + gp * (1.0 - s))).astype(BF16)
        gup[at] = (gh * (gp * s)).astype(BF16)

    def sums(k, g):
        at = slice(g * size, (g + 1) * size)

        def one(f):
            feats = pl.ds(pl.multiple_of(f * width, width), width)
            if k == 0:
                return jnp.dot(hidden[at], wd[:, feats], preferred_element_type=F32)
            return lax.dot_general(
                ggp[at], wg[feats, :], over_cols, preferred_element_type=F32
            ) + lax.dot_general(gup[at], wu[feats, :], over_cols, preferred_element_type=F32)

        for ax in range(2):
            sib_src[k, ax, at] = one(ax * 2 + 1 - c).astype(BF16)
        for j in (2 * g, 2 * g + 1):
            part = pl.ds(j * block, block)
            send(RSIB, k, j, sib_src.at[k, :, part], sib_dst.at[k, :, part], s_dev)
        for ax in range(2):
            keep[k, ax, at] = one(ax * 2 + c)

    def pair_sum(k, j, at_x, at_y):
        where = pl.ds(pl.multiple_of(j * block + at_y * cap, cap), cap)
        return keep[k, at_x, where] + sib_dst[k, at_x, where].astype(F32)

    def r1(q):
        k, j = q // n_lang, q % n_lang
        part = pl.ds(j * block, block)
        recv(RSIB, k, j, sib_dst.at[k, :, part], s_dev)
        diag_src[k, j] = pair_sum(k, j, nx, ny).astype(BF16)
        top, low = pl.ds(0, half), pl.ds(half, half)
        send(RDA, k, j, diag_src.at[k, j, top], diag_dst.at[k, j, top], y_dev)
        send(RDB, k, j, diag_src.at[k, j, low], diag_dst.at[k, j, low], x_dev)

    def r2(q):
        k, j = q // n_lang, q % n_lang
        top, low = pl.ds(0, half), pl.ds(half, half)
        recv(RDA, k, j, diag_dst.at[k, j, top], y_dev)
        to_x = pair_sum(k, j, nx, y)
        nx_src[k, j, top] = (to_x[:half] + diag_dst[k, j, top].astype(F32)).astype(BF16)
        nx_src[k, j, low] = to_x[half:].astype(BF16)
        send(RX, k, j, nx_src.at[k, j], nx_dst.at[k, j], x_dev)
        recv(RDB, k, j, diag_dst.at[k, j, low], x_dev)
        to_y = pair_sum(k, j, x, ny)
        ny_src[k, j, top] = to_y[:half].astype(BF16)
        ny_src[k, j, low] = (to_y[half:] + diag_dst[k, j, low].astype(F32)).astype(BF16)
        send(RY, k, j, ny_src.at[k, j], ny_dst.at[k, j], y_dev)

    def r3(q):
        k, j = q // n_lang, q % n_lang
        recv(RX, k, j, nx_dst.at[k, j], x_dev)
        recv(RY, k, j, ny_dst.at[k, j], y_dev)
        total = pair_sum(k, j, x, y) + nx_dst[k, j].astype(F32) + ny_dst[k, j].astype(F32)
        if j:
            back_src[k, j] = total.astype(BF16)
            send(RZ, k, j, back_src.at[k, j], back.at[k, z], z_dev[j])
        else:
            back[k, z] = total.astype(BF16)

    def home(k, out_ref):
        for j in range(1, n_lang):
            recv(RZ, k, j, back.at[k, plane[j]], z_dev[j])
        flat = back[k].reshape(n_lang * cap, width)
        out_ref[...] = jnp.dot(to_slot, flat, preferred_element_type=F32).astype(BF16)

    stores = []

    def store(src, dst, n):
        going = pltpu.make_async_copy(src, dst, local_sem.at[n])
        going.start()
        stores.append(going)

    g0(0)
    g0(1), g1(0)
    g0(2), g1(1), g2(0)
    g0(3), g1(2), g2(1), g3(0)
    g0(4), g1(3), g2(2), g3(1)
    for load in loads:
        load.wait()
    forward(0)
    g0(5), g1(4), g2(3), g3(2)
    g0(6), g1(5), g2(4), g3(3)
    forward(1)
    g0(7), g1(6), g2(5), g3(4)
    sums(0, 0)
    g1(7), g2(6), g3(5)
    r1(0), r1(1)
    backward(0)
    g2(7), g3(6)
    sums(0, 1)
    g3(7)
    r2(0), r2(1), r1(2), r1(3)
    backward(1)
    store(rows, rows_hbm, 3)
    store(hidden, hid_hbm, 4)
    store(ggp, ggp_hbm, 5)
    store(gup, gup_hbm, 6)
    r3(0), r3(1), r2(2), r2(3)
    sums(1, 0)
    r3(2), r3(3), r1(4), r1(5)
    sums(1, 1)
    r2(4), r2(5), r1(6), r1(7)
    r3(4), r3(5), r2(6), r2(7)
    home(0, y_ref)
    r3(6), r3(7)
    home(1, yg_ref)
    for going in started:
        going.wait_send()
    for going in stores:
        going.wait()


def weight_grad_kernel(rows_ref, grads_ref, hid_ref, ggp_ref, gup_ref, dg_ref, du_ref, dd_ref):
    over_rows = (((0,), (0,)), ((), ()))
    here = rows_ref[0, 0]
    dg_ref[0] = lax.dot_general(here, ggp_ref[...], over_rows, preferred_element_type=F32).astype(BF16)
    du_ref[0] = lax.dot_general(here, gup_ref[...], over_rows, preferred_element_type=F32).astype(BF16)
    dd_ref[0] = lax.dot_general(
        hid_ref[...], grads_ref[0, 0], over_rows, preferred_element_type=F32
    ).astype(BF16)


def fused_body(
    tokens, labels, domain_ids, domain_weights, cotangent, gate_weight, up_weight, down_weight
):
    n_lang = lax.axis_size("expert") // SPLIT
    n_feat = lax.axis_size("tensor")
    n_tok, width = tokens.shape
    cap = 2 * n_tok // n_lang
    n_rows = n_lang * SPLIT * cap
    feats = n_feat * width
    hid = gate_weight.shape[2]
    vmem = pl.BlockSpec(memory_space=pltpu.VMEM)
    hbm = pl.BlockSpec(memory_space=pl.ANY)
    out = jax.ShapeDtypeStruct((n_tok, width), BF16)
    act = jax.ShapeDtypeStruct((n_rows, hid), BF16)
    slab = pltpu.VMEM((2, n_lang, cap, width), BF16)
    y, yg, rows, hidden, ggp, gup = pl.pallas_call(
        expert_kernel,
        out_shape=(
            out, out, jax.ShapeDtypeStruct((2, n_feat, n_rows, width), BF16), act, act, act
        ),
        in_specs=[vmem] * 5 + [hbm] * 3,
        out_specs=(vmem, vmem, hbm, hbm, hbm, hbm),
        scratch_shapes=[
            pltpu.VMEM((feats, hid), BF16),
            pltpu.VMEM((feats, hid), BF16),
            pltpu.VMEM((hid, feats), BF16),
            pltpu.VMEM((n_lang, 2, cap, width), BF16),
            pltpu.VMEM((2, n_feat, n_rows, width), BF16),
            pltpu.VMEM((n_rows, hid), F32),
            pltpu.VMEM((n_rows, hid), F32),
            pltpu.VMEM((n_rows, hid), BF16),
            pltpu.VMEM((n_rows, hid), BF16),
            pltpu.VMEM((n_rows, hid), BF16),
            pltpu.VMEM((2, 2, n_rows, width), F32),
            pltpu.VMEM((2, 2, n_rows, width), BF16),
            pltpu.VMEM((2, 2, n_rows, width), BF16),
            slab, slab, slab, slab, slab, slab, slab, slab,
            pltpu.SemaphoreType.DMA((KINDS, 2, n_lang)),
            pltpu.SemaphoreType.DMA((KINDS, 2, n_lang)),
            pltpu.SemaphoreType.DMA((7,)),
        ],
        compiler_params=pltpu.CompilerParams(
            collective_id=0, has_side_effects=True, vmem_limit_bytes=48 * 2**20
        ),
        name="expert_layer",
    )(
        tokens, cotangent, labels, domain_ids.reshape(1, n_tok),
        domain_weights.reshape(1, -1), gate_weight, up_weight, down_weight,
    )
    whole_act = pl.BlockSpec((n_rows, hid), lambda f: (0, 0))
    dg, du, dd = pl.pallas_call(
        weight_grad_kernel,
        grid=(n_feat,),
        out_shape=(
            jax.ShapeDtypeStruct(gate_weight.shape, BF16),
            jax.ShapeDtypeStruct(up_weight.shape, BF16),
            jax.ShapeDtypeStruct(down_weight.shape, BF16),
        ),
        in_specs=[
            pl.BlockSpec((1, 1, n_rows, width), lambda f: (0, f, 0, 0)),
            pl.BlockSpec((1, 1, n_rows, width), lambda f: (1, f, 0, 0)),
            whole_act, whole_act, whole_act,
        ],
        out_specs=(
            pl.BlockSpec((1, width, hid), lambda f: (0, f, 0)),
            pl.BlockSpec((1, width, hid), lambda f: (0, f, 0)),
            pl.BlockSpec((1, hid, width), lambda f: (0, 0, f)),
        ),
        compiler_params=pltpu.CompilerParams(vmem_limit_bytes=32 * 2**20),
        name="weight_grads",
    )(rows, rows, hidden, ggp, gup)
    return (y, yg, dg, du, dd)


def solution(mesh):
    n_lang = mesh.shape["expert"] // SPLIT
    fits = n_lang == 4 and mesh.shape["tensor"] == 4
    return jax.shard_map(
        fused_body if fits else body,
        mesh=mesh,
        in_specs=(
            P("expert", "tensor"),
            P("expert", None),
            P("expert"),
            P(),
            P("expert", "tensor"),
            P("expert", None, "tensor"),
            P("expert", None, "tensor"),
            P("expert", "tensor", None),
        ),
        out_specs=(
            P("expert", "tensor"),
            P("expert", "tensor"),
            P("expert", None, "tensor"),
            P("expert", None, "tensor"),
            P("expert", "tensor", None),
        ),
        check_vma=False,
    )
```

```python
import jax
import jax.numpy as jnp
from jax import lax
from jax.experimental import pallas as pl
from jax.experimental.pallas import tpu as pltpu
from jax.sharding import PartitionSpec as P

SPLIT = 2
F32 = jnp.float32
BF16 = jnp.bfloat16
MESH = pl.DeviceIdType.MESH
(
    ZOUT, XOWN, YOWN, SOWN, FWDA, FWDB, SPX, SPY, SPD,
    RSIB, RDA, RDB, RX, RY, RZ, KINDS,
) = range(16)


def partner(value, axis, stride):
    return lax.ppermute(value, axis, [(i, i ^ 1 << stride) for i in range(lax.axis_size(axis))])


def silu_parts(gate_pre):
    squash = jax.nn.sigmoid(gate_pre)
    return (squash, gate_pre * squash)


def body(
    tokens, labels, domain_ids, domain_weights, cotangent, gate_weight, up_weight, down_weight
):
    n_expert = lax.axis_size("expert")
    tok_rows = tokens.shape[0]
    experts_all = n_expert // SPLIT
    capacity = 2 * tok_rows // experts_all
    half_cap = capacity // 2
    parity = lax.axis_index("expert") % 2
    lang_label = labels[:, 0]
    dom_hot = (
        domain_ids[:, None] == jnp.arange(domain_weights.shape[0], dtype=jnp.int32)[None, :]
    ).astype(jnp.float32)
    tok_scale = jnp.sum(dom_hot * domain_weights[None, :], axis=1)
    grad_rows = (tok_scale[:, None] * cotangent.astype(jnp.float32)).astype(jnp.bfloat16)
    lab_hot = (lang_label[:, None] == jnp.arange(experts_all, dtype=jnp.int32)[None, :]).astype(
        jnp.float32
    )
    row_ids = jnp.arange(tok_rows, dtype=jnp.int32)
    earlier = (row_ids[None, :] < row_ids[:, None]).astype(jnp.float32)
    before = jnp.dot(earlier, lab_hot, precision=lax.Precision.HIGHEST)
    slot_pos = jnp.sum(before * lab_hot, axis=1).astype(jnp.int32)
    target_row = lang_label * capacity + slot_pos
    sources = jnp.stack((tokens, grad_rows))
    sources = lax.all_gather(sources, "tensor", axis=2, tiled=True)
    slot_ids = jnp.arange(n_expert * capacity, dtype=jnp.int32)
    dispatch_map = (slot_ids[:, None] // capacity // SPLIT == lang_label[None, :]) & (
        slot_ids[:, None] % capacity == slot_pos[None, :]
    )
    dispatch_map = dispatch_map.astype(jnp.bfloat16)
    outbound = jnp.einsum(
        "rt,ktw->krw", dispatch_map, sources, preferred_element_type=jnp.float32
    ).astype(jnp.bfloat16)
    outbound = outbound.reshape(2, n_expert, capacity, sources.shape[2])
    arrived = lax.all_to_all(outbound, "expert", split_axis=1, concat_axis=1, tiled=True)
    rows_all = n_expert * capacity
    feat_width = arrived.shape[3]
    routed = arrived[0].reshape(rows_all, feat_width)
    routed_grad = arrived[1].reshape(rows_all, feat_width)
    w_gate = gate_weight[0]
    w_up = up_weight[0]
    w_down = down_weight[0]
    contract_rows = (((0,), (0,)), ((), ()))
    contract_cols = (((1,), (1,)), ((), ()))
    gate_pre = jnp.dot(routed, w_gate, preferred_element_type=jnp.float32)
    up_pre = jnp.dot(routed, w_up, preferred_element_type=jnp.float32)
    squash, activated = silu_parts(gate_pre)
    hidden = (activated * up_pre).astype(jnp.bfloat16)
    out_part = jnp.dot(hidden, w_down, preferred_element_type=jnp.float32)
    grad_hidden = lax.dot_general(
        routed_grad, w_down, contract_cols, preferred_element_type=jnp.float32
    )
    grad_gate_pre = (grad_hidden * up_pre * squash * (1.0 + gate_pre * (1.0 - squash))).astype(
        jnp.bfloat16
    )
    grad_up_pre = (grad_hidden * activated).astype(jnp.bfloat16)
    gate_grad = lax.dot_general(
        routed, grad_gate_pre, contract_rows, preferred_element_type=jnp.float32
    ).astype(jnp.bfloat16)[None]
    up_grad = lax.dot_general(
        routed, grad_up_pre, contract_rows, preferred_element_type=jnp.float32
    ).astype(jnp.bfloat16)[None]
    down_grad = lax.dot_general(
        hidden, routed_grad, contract_rows, preferred_element_type=jnp.float32
    ).astype(jnp.bfloat16)[None]
    input_part = lax.dot_general(
        grad_gate_pre, w_gate, contract_cols, preferred_element_type=jnp.float32
    ) + lax.dot_general(grad_up_pre, w_up, contract_cols, preferred_element_type=jnp.float32)
    out_part = out_part.reshape(n_expert, capacity, feat_width)
    input_part = input_part.reshape(n_expert, capacity, feat_width)
    out_share, input_share = (
        lax.psum_scatter(out_part, "tensor", scatter_dimension=2, tiled=True),
        lax.psum_scatter(input_part, "tensor", scatter_dimension=2, tiled=True),
    )
    partial_value = jnp.stack((out_share, input_share))
    kept = jnp.where(parity == 0, partial_value[:, :, :half_cap], partial_value[:, :, half_cap:])
    handed = jnp.where(parity == 0, partial_value[:, :, half_cap:], partial_value[:, :, :half_cap])
    summed = kept + partner(handed, "expert", 0)
    going_back = summed.astype(jnp.bfloat16)
    returned = lax.all_to_all(going_back, "expert", split_axis=1, concat_axis=1, tiled=True)
    home_ids = jnp.arange(n_expert * half_cap, dtype=jnp.int32)
    home_map = (home_ids[:, None] == target_row[None, :]).astype(jnp.bfloat16)
    flat_back = returned.reshape(2, n_expert * half_cap, returned.shape[3])
    gathered_home = jnp.einsum(
        "rt,krw->ktw", home_map, flat_back, preferred_element_type=jnp.float32
    ).astype(jnp.bfloat16)
    return (gathered_home[0], gathered_home[1], gate_grad, up_grad, down_grad)


def expert_kernel(
    tok_hbm, cot_hbm, lab_hbm, dom_hbm, dw_hbm, wg_hbm, wu_hbm, wd_hbm,
    map_hbm, back_hbm, dg_hbm, du_hbm, dd_hbm,
    slot_map, back, dg, du, dd, tok_ref, cot_ref, lab_ref, dom_ref, dw_ref, wg, wu, wd, slots, rows, gate_pre, up_pre, hidden, ggp, gup, keep,
    sib_src, sib_dst, diag_src, diag_dst, nx_src, nx_dst, ny_src, ny_dst,
    back_src, send_sem, recv_sem, local_sem,
):
    n_tok, width = tok_ref.shape
    n_lang = slots.shape[0]
    cap = slots.shape[2]
    half = cap // 2
    block = 2 * cap
    ei = lax.axis_index("expert")
    ti = lax.axis_index("tensor")
    z, y = ei // 2, ei % 2
    x, c = ti // 2, ti % 2
    nx, ny = 1 - x, 1 - y
    tix = nx * 2 + c
    tis = x * 2 + 1 - c
    tixs = nx * 2 + 1 - c
    plane = [z, z + 1 - 2 * (z % 2), (z + 2) % 4, 3 - z]
    x_dev, y_dev, s_dev = (ei, tix), (z * 2 + ny, ti), (ei, tis)
    z_dev = [(plane[j] * 2 + y, ti) for j in range(n_lang)]

    loads = [
        pltpu.make_async_copy(src, dst, local_sem.at[n])
        for n, (src, dst) in enumerate((
            (lab_hbm, lab_ref), (tok_hbm, tok_ref), (dom_hbm, dom_ref), (dw_hbm, dw_ref),
            (cot_hbm, cot_ref), (wg_hbm.at[0], wg), (wu_hbm.at[0], wu), (wd_hbm.at[0], wd),
        ))
    ]
    barrier = pltpu.get_barrier_semaphore()
    others = [x_dev, y_dev, s_dev] + z_dev[1:]
    for dev in others:
        pl.semaphore_signal(barrier, inc=1, device_id=dev, device_id_type=MESH)
    for copy in loads:
        copy.start()

    started = []

    def copy(kind, k, j, src, dst, dev):
        return pltpu.make_async_remote_copy(
            src_ref=src, dst_ref=dst, send_sem=send_sem.at[kind, k, j],
            recv_sem=recv_sem.at[kind, k, j], device_id=dev, device_id_type=MESH,
        )

    def send(kind, k, j, src, dst, dev):
        going = copy(kind, k, j, src, dst, dev)
        going.start()
        started.append(going)

    def recv(kind, k, j, dst, dev):
        copy(kind, k, j, dst, dst, dev).wait_recv()

    def piece(k, f, j, row_y, part=None):
        first = j * block + row_y * cap
        size = cap
        if part is not None:
            first = first + part * half
            size = half
        return rows.at[k, f, pl.ds(pl.multiple_of(first, half), size)]

    loads[0].wait()
    lane = lax.broadcasted_iota(jnp.int32, (n_tok, n_tok), 1)
    sub = lax.broadcasted_iota(jnp.int32, (n_tok, n_tok), 0)

    def column(row_ref):
        wide = jnp.broadcast_to(row_ref[...].astype(F32), (n_tok, n_tok))
        return jnp.sum(jnp.where(lane == sub, wide, 0.0), axis=1, keepdims=True)

    lab = column(lab_ref)
    lab_hot = jnp.where(lane.astype(F32) == lab, 1.0, 0.0)
    earlier = jnp.where(lane < sub, 1.0, 0.0).astype(BF16)
    before = jnp.dot(earlier, lab_hot.astype(BF16), preferred_element_type=F32)
    pos = jnp.sum(before * lab_hot, axis=1, keepdims=True)
    target = lab * cap + pos
    slot_lane = lax.broadcasted_iota(jnp.int32, (n_tok, n_lang * cap), 1).astype(F32)
    to_slot = jnp.where(slot_lane == target, 1.0, 0.0).astype(BF16)
    slot_map[...] = to_slot
    map_store = pltpu.make_async_copy(slot_map, map_hbm, local_sem.at[21])
    map_store.start()
    over_tokens = (((0,), (0,)), ((), ()))

    def pack(k, source):
        packed = lax.dot_general(
            to_slot, source, over_tokens, preferred_element_type=F32
        ).astype(BF16)
        for e in range(n_lang):
            slots[e, k] = packed[e * cap:(e + 1) * cap]

    def exchange(k):
        for j in range(1, n_lang):
            send(ZOUT, k, j, slots.at[plane[j], k], piece(k, ti, j, y), z_dev[j])
        piece(k, ti, 0, y)[...] = slots[z, k]

    loads[1].wait()
    pack(0, tok_ref[...])
    pl.semaphore_wait(barrier, len(others))
    exchange(0)
    for load in loads[2:5]:
        load.wait()
    n_dom = dw_ref.shape[1]
    dom_lane = lax.broadcasted_iota(jnp.int32, (n_tok, n_dom), 1).astype(F32)
    dw_row = jnp.broadcast_to(dw_ref[...], (n_tok, n_dom))
    scale = jnp.sum(
        jnp.where(dom_lane == column(dom_ref), dw_row, 0.0), axis=1, keepdims=True
    )

    order = [(0, 0), (1, 0), (0, 1), (0, 2), (0, 3), (1, 1), (1, 2), (1, 3)]

    def g0(q):
        k, j = order[q]
        own = piece(k, ti, j, y)
        if j:
            recv(ZOUT, k, j, own, z_dev[j])
        send(XOWN, k, j, own, own, x_dev)
        send(YOWN, k, j, own, own, y_dev)
        send(SOWN, k, j, own, own, s_dev)

    def g1(q):
        k, j = order[q]
        from_x, from_y = piece(k, tix, j, y), piece(k, ti, j, ny)
        recv(XOWN, k, j, from_x, x_dev)
        part = piece(k, tix, j, y, 0)
        send(FWDA, k, j, part, part, y_dev)
        send(SPX, k, j, from_x, from_x, s_dev)
        recv(YOWN, k, j, from_y, y_dev)
        part = piece(k, ti, j, ny, 1)
        send(FWDB, k, j, part, part, x_dev)
        send(SPY, k, j, from_y, from_y, s_dev)

    def g2(q):
        k, j = order[q]
        recv(FWDA, k, j, piece(k, tix, j, ny, 0), y_dev)
        recv(FWDB, k, j, piece(k, tix, j, ny, 1), x_dev)
        diag = piece(k, tix, j, ny)
        send(SPD, k, j, diag, diag, s_dev)

    def g3(q):
        k, j = order[q]
        recv(SOWN, k, j, piece(k, tis, j, y), s_dev)
        recv(SPX, k, j, piece(k, tixs, j, y), s_dev)
        recv(SPY, k, j, piece(k, tis, j, ny), s_dev)
        recv(SPD, k, j, piece(k, tixs, j, ny), s_dev)

    size = 2 * block
    n_feat = rows.shape[1]
    over_cols = (((1,), (1,)), ((), ()))

    def all_feats(k, g):
        return jnp.concatenate(
            [rows[k, f, g * size:(g + 1) * size] for f in range(n_feat)], axis=1
        )

    def forward(g):
        at = slice(g * size, (g + 1) * size)
        here = all_feats(0, g)
        gp = jnp.dot(here, wg[...], preferred_element_type=F32)
        up = jnp.dot(here, wu[...], preferred_element_type=F32)
        gate_pre[at] = gp
        up_pre[at] = up
        hidden[at] = (gp * jax.nn.sigmoid(gp) * up).astype(BF16)

    def backward(g):
        at = slice(g * size, (g + 1) * size)
        gh = lax.dot_general(all_feats(1, g), wd[...], over_cols, preferred_element_type=F32)
        gp, up = gate_pre[at], up_pre[at]
        s = jax.nn.sigmoid(gp)
        ggp[at] = (gh * up * s * (1.0 + gp * (1.0 - s))).astype(BF16)
        gup[at] = (gh * (gp * s)).astype(BF16)

    def sums(k, g):
        at = slice(g * size, (g + 1) * size)

        def one(f):
            feats = pl.ds(pl.multiple_of(f * width, width), width)
            if k == 0:
                return jnp.dot(hidden[at], wd[:, feats], preferred_element_type=F32)
            return lax.dot_general(
                ggp[at], wg[feats, :], over_cols, preferred_element_type=F32
            ) + lax.dot_general(gup[at], wu[feats, :], over_cols, preferred_element_type=F32)

        for ax in range(2):
            sib_src[k, ax, at] = one(ax * 2 + 1 - c).astype(BF16)
        for j in (2 * g, 2 * g + 1):
            part = pl.ds(j * block, block)
            send(RSIB, k, j, sib_src.at[k, :, part], sib_dst.at[k, :, part], s_dev)
        for ax in range(2):
            keep[k, ax, at] = one(ax * 2 + c)

    def pair_sum(k, j, at_x, at_y):
        where = pl.ds(pl.multiple_of(j * block + at_y * cap, cap), cap)
        return keep[k, at_x, where] + sib_dst[k, at_x, where].astype(F32)

    def r1(q):
        k, j = q // n_lang, q % n_lang
        part = pl.ds(j * block, block)
        recv(RSIB, k, j, sib_dst.at[k, :, part], s_dev)
        diag_src[k, j] = pair_sum(k, j, nx, ny).astype(BF16)
        top, low = pl.ds(0, half), pl.ds(half, half)
        send(RDA, k, j, diag_src.at[k, j, top], diag_dst.at[k, j, top], y_dev)
        send(RDB, k, j, diag_src.at[k, j, low], diag_dst.at[k, j, low], x_dev)

    def r2(q):
        k, j = q // n_lang, q % n_lang
        top, low = pl.ds(0, half), pl.ds(half, half)
        recv(RDA, k, j, diag_dst.at[k, j, top], y_dev)
        to_x = pair_sum(k, j, nx, y)
        nx_src[k, j, top] = (to_x[:half] + diag_dst[k, j, top].astype(F32)).astype(BF16)
        nx_src[k, j, low] = to_x[half:].astype(BF16)
        send(RX, k, j, nx_src.at[k, j], nx_dst.at[k, j], x_dev)
        recv(RDB, k, j, diag_dst.at[k, j, low], x_dev)
        to_y = pair_sum(k, j, x, ny)
        ny_src[k, j, top] = to_y[:half].astype(BF16)
        ny_src[k, j, low] = (to_y[half:] + diag_dst[k, j, low].astype(F32)).astype(BF16)
        send(RY, k, j, ny_src.at[k, j], ny_dst.at[k, j], y_dev)

    def r3(q):
        k, j = q // n_lang, q % n_lang
        recv(RX, k, j, nx_dst.at[k, j], x_dev)
        recv(RY, k, j, ny_dst.at[k, j], y_dev)
        total = pair_sum(k, j, x, y) + nx_dst[k, j].astype(F32) + ny_dst[k, j].astype(F32)
        if j:
            back_src[k, j] = total.astype(BF16)
            send(RZ, k, j, back_src.at[k, j], back.at[k, z], z_dev[j])
        else:
            back[k, z] = total.astype(BF16)

    over_rows = (((0,), (0,)), ((), ()))

    stores = []

    def store(src, dst):
        going = pltpu.make_async_copy(src, dst, local_sem.at[8 + len(stores)])
        going.start()
        stores.append(going)

    def weight_grad(which, f):
        at = slice(f * width, (f + 1) * width)
        if which == 2:
            dd[0, :, at] = lax.dot_general(
                hidden[...], rows[1, f], over_rows, preferred_element_type=F32
            ).astype(BF16)
            store(dd.at[0, :, at], dd_hbm.at[0, :, at])
        else:
            out, grad, out_hbm = ((dg, ggp, dg_hbm), (du, gup, du_hbm))[which]
            out[0, at] = lax.dot_general(
                rows[0, f], grad[...], over_rows, preferred_element_type=F32
            ).astype(BF16)
            store(out.at[0, at], out_hbm.at[0, at])

    g0(0)
    pack(1, (scale * cot_ref[...].astype(F32)).astype(BF16))
    exchange(1)
    g0(1), g1(0)
    g0(2), g1(1), g2(0)
    g0(3), g1(2), g2(1), g3(0)
    g0(4), g1(3), g2(2), g3(1)
    for load in loads[5:]:
        load.wait()
    g0(5), g1(4), g2(3), g3(2)
    g0(6)
    forward(0)
    g1(5), g2(4), g3(3), g0(7)
    sums(0, 0)
    g1(6), g2(5), g3(4), r1(0)
    forward(1)
    g1(7), g2(6), g3(5), r1(1)
    backward(0)
    r2(0), r2(1)
    sums(0, 1)
    g2(7), g3(6), g3(7), r1(2), r1(3)
    sums(1, 0)
    r3(0), r3(1), r2(2), r2(3), r1(4), r1(5)
    backward(1)
    r3(2), r3(3), r2(4), r2(5)
    sums(1, 1)
    r1(6), r1(7), r3(4), r3(5)
    weight_grad(2, 0), weight_grad(2, 1)
    r2(6), r2(7)
    for f in range(2, n_feat):
        weight_grad(2, f)
    weight_grad(0, 0)
    r3(6), r3(7)
    for f in range(1, n_feat):
        weight_grad(0, f)
    for f in range(n_feat):
        weight_grad(1, f)
    for k in range(2):
        for j in range(1, n_lang):
            recv(RZ, k, j, back.at[k, plane[j]], z_dev[j])
    store(back, back_hbm)
    for going in started:
        going.wait_send()
    for going in stores + [map_store]:
        going.wait()


def home_kernel(
    map_hbm, back_hbm, dg_in, du_in, dd_in, y_ref, yg_ref, dg_out, du_out, dd_out,
    slot_map, back, dg, du, dd, sem,
):
    first = [
        pltpu.make_async_copy(map_hbm, slot_map, sem.at[0]),
        pltpu.make_async_copy(back_hbm, back, sem.at[1]),
    ]
    into, outof = [], []
    for src, held, dst in ((dg_in, dg, dg_out), (du_in, du, du_out), (dd_in, dd, dd_out)):
        step = src.shape[1] // 4
        for n in range(4):
            part = pl.ds(n * step, step)
            at = 2 + 2 * len(into)
            into.append(pltpu.make_async_copy(src.at[0, part], held.at[0, part], sem.at[at]))
            outof.append(pltpu.make_async_copy(held.at[0, part], dst.at[0, part], sem.at[at + 1]))
    for going in first + into:
        going.start()
    for going in first:
        going.wait()
    _, n_lang, cap, width = back.shape
    for k, out_ref in enumerate((y_ref, yg_ref)):
        flat = back[k].reshape(n_lang * cap, width)
        out_ref[...] = jnp.dot(slot_map[...], flat, preferred_element_type=F32).astype(BF16)
    for arriving, leaving in zip(into, outof):
        arriving.wait()
        leaving.start()
    for going in outof:
        going.wait()


def fused_body(
    tokens, labels, domain_ids, domain_weights, cotangent, gate_weight, up_weight, down_weight
):
    n_lang = lax.axis_size("expert") // SPLIT
    n_feat = lax.axis_size("tensor")
    n_tok, width = tokens.shape
    cap = 2 * n_tok // n_lang
    n_rows = n_lang * SPLIT * cap
    feats = n_feat * width
    hid = gate_weight.shape[2]
    vmem = pl.BlockSpec(memory_space=pltpu.VMEM)
    hbm = pl.BlockSpec(memory_space=pltpu.HBM)
    out = jax.ShapeDtypeStruct((n_tok, width), BF16)
    slab = pltpu.VMEM((2, n_lang, cap, width), BF16)
    grads = tuple(
        jax.ShapeDtypeStruct(w.shape, BF16) for w in (gate_weight, up_weight, down_weight)
    )
    parts = pl.pallas_call(
        expert_kernel,
        out_shape=(
            jax.ShapeDtypeStruct((n_tok, n_lang * cap), BF16),
            jax.ShapeDtypeStruct((2, n_lang, cap, width), BF16),
        ) + grads,
        in_specs=[hbm] * 8,
        out_specs=(hbm,) * 5,
        scratch_shapes=[
            pltpu.VMEM((n_tok, n_lang * cap), BF16),
            slab,
            pltpu.VMEM(gate_weight.shape, BF16),
            pltpu.VMEM(up_weight.shape, BF16),
            pltpu.VMEM(down_weight.shape, BF16),
            pltpu.VMEM((n_tok, width), BF16),
            pltpu.VMEM((n_tok, width), BF16),
            pltpu.VMEM((1, n_tok), jnp.int32),
            pltpu.VMEM((1, n_tok), jnp.int32),
            pltpu.VMEM((1, domain_weights.shape[0]), F32),
            pltpu.VMEM((feats, hid), BF16),
            pltpu.VMEM((feats, hid), BF16),
            pltpu.VMEM((hid, feats), BF16),
            pltpu.VMEM((n_lang, 2, cap, width), BF16),
            pltpu.VMEM((2, n_feat, n_rows, width), BF16),
            pltpu.VMEM((n_rows, hid), F32),
            pltpu.VMEM((n_rows, hid), F32),
            pltpu.VMEM((n_rows, hid), BF16),
            pltpu.VMEM((n_rows, hid), BF16),
            pltpu.VMEM((n_rows, hid), BF16),
            pltpu.VMEM((2, 2, n_rows, width), F32),
            pltpu.VMEM((2, 2, n_rows, width), BF16),
            pltpu.VMEM((2, 2, n_rows, width), BF16),
            slab, slab, slab, slab, slab, slab, slab,
            pltpu.SemaphoreType.DMA((KINDS, 2, n_lang)),
            pltpu.SemaphoreType.DMA((KINDS, 2, n_lang)),
            pltpu.SemaphoreType.DMA((22,)),
        ],
        compiler_params=pltpu.CompilerParams(
            collective_id=0, has_side_effects=True, vmem_limit_bytes=58 * 2**20
        ),
        name="expert_layer",
    )(
        tokens, cotangent, labels.reshape(1, n_tok), domain_ids.reshape(1, n_tok),
        domain_weights.reshape(1, -1), gate_weight, up_weight, down_weight,
    )
    return pl.pallas_call(
        home_kernel,
        out_shape=(out, out) + grads,
        in_specs=[hbm] * 5,
        out_specs=(vmem, vmem, hbm, hbm, hbm),
        scratch_shapes=[
            pltpu.VMEM((n_tok, n_lang * cap), BF16),
            slab,
            pltpu.VMEM(gate_weight.shape, BF16),
            pltpu.VMEM(up_weight.shape, BF16),
            pltpu.VMEM(down_weight.shape, BF16),
            pltpu.SemaphoreType.DMA((26,)),
        ],
        compiler_params=pltpu.CompilerParams(vmem_limit_bytes=58 * 2**20),
        name="home",
    )(*parts)


def solution(mesh):
    n_lang = mesh.shape["expert"] // SPLIT
    fits = n_lang == 4 and mesh.shape["tensor"] == 4
    return jax.shard_map(
        fused_body if fits else body,
        mesh=mesh,
        in_specs=(
            P("expert", "tensor"),
            P("expert", None),
            P("expert"),
            P(),
            P("expert", "tensor"),
            P("expert", None, "tensor"),
            P("expert", None, "tensor"),
            P("expert", "tensor", None),
        ),
        out_specs=(
            P("expert", "tensor"),
            P("expert", "tensor"),
            P("expert", None, "tensor"),
            P("expert", None, "tensor"),
            P("expert", "tensor", None),
        ),
        check_vma=False,
    )
```

```python
import jax
import jax.numpy as jnp
from jax import lax
from jax.experimental import pallas as pl
from jax.experimental.pallas import tpu as pltpu
from jax.sharding import PartitionSpec as P

SPLIT = 2
F32 = jnp.float32
BF16 = jnp.bfloat16
MESH = pl.DeviceIdType.MESH
(
    ZOUT, XOWN, YOWN, SOWN, FWDA, FWDB, SPX, SPY, SPD,
    RSIB, RDA, RDB, RX, RY, RZ, KINDS,
) = range(16)


def partner(value, axis, stride):
    return lax.ppermute(value, axis, [(i, i ^ 1 << stride) for i in range(lax.axis_size(axis))])


def silu_parts(gate_pre):
    squash = jax.nn.sigmoid(gate_pre)
    return (squash, gate_pre * squash)


def body(
    tokens, labels, domain_ids, domain_weights, cotangent, gate_weight, up_weight, down_weight
):
    n_expert = lax.axis_size("expert")
    tok_rows = tokens.shape[0]
    experts_all = n_expert // SPLIT
    capacity = 2 * tok_rows // experts_all
    half_cap = capacity // 2
    parity = lax.axis_index("expert") % 2
    lang_label = labels[:, 0]
    dom_hot = (
        domain_ids[:, None] == jnp.arange(domain_weights.shape[0], dtype=jnp.int32)[None, :]
    ).astype(jnp.float32)
    tok_scale = jnp.sum(dom_hot * domain_weights[None, :], axis=1)
    grad_rows = (tok_scale[:, None] * cotangent.astype(jnp.float32)).astype(jnp.bfloat16)
    lab_hot = (lang_label[:, None] == jnp.arange(experts_all, dtype=jnp.int32)[None, :]).astype(
        jnp.float32
    )
    row_ids = jnp.arange(tok_rows, dtype=jnp.int32)
    earlier = (row_ids[None, :] < row_ids[:, None]).astype(jnp.float32)
    before = jnp.dot(earlier, lab_hot, precision=lax.Precision.HIGHEST)
    slot_pos = jnp.sum(before * lab_hot, axis=1).astype(jnp.int32)
    target_row = lang_label * capacity + slot_pos
    sources = jnp.stack((tokens, grad_rows))
    sources = lax.all_gather(sources, "tensor", axis=2, tiled=True)
    slot_ids = jnp.arange(n_expert * capacity, dtype=jnp.int32)
    dispatch_map = (slot_ids[:, None] // capacity // SPLIT == lang_label[None, :]) & (
        slot_ids[:, None] % capacity == slot_pos[None, :]
    )
    dispatch_map = dispatch_map.astype(jnp.bfloat16)
    outbound = jnp.einsum(
        "rt,ktw->krw", dispatch_map, sources, preferred_element_type=jnp.float32
    ).astype(jnp.bfloat16)
    outbound = outbound.reshape(2, n_expert, capacity, sources.shape[2])
    arrived = lax.all_to_all(outbound, "expert", split_axis=1, concat_axis=1, tiled=True)
    rows_all = n_expert * capacity
    feat_width = arrived.shape[3]
    routed = arrived[0].reshape(rows_all, feat_width)
    routed_grad = arrived[1].reshape(rows_all, feat_width)
    w_gate = gate_weight[0]
    w_up = up_weight[0]
    w_down = down_weight[0]
    contract_rows = (((0,), (0,)), ((), ()))
    contract_cols = (((1,), (1,)), ((), ()))
    gate_pre = jnp.dot(routed, w_gate, preferred_element_type=jnp.float32)
    up_pre = jnp.dot(routed, w_up, preferred_element_type=jnp.float32)
    squash, activated = silu_parts(gate_pre)
    hidden = (activated * up_pre).astype(jnp.bfloat16)
    out_part = jnp.dot(hidden, w_down, preferred_element_type=jnp.float32)
    grad_hidden = lax.dot_general(
        routed_grad, w_down, contract_cols, preferred_element_type=jnp.float32
    )
    grad_gate_pre = (grad_hidden * up_pre * squash * (1.0 + gate_pre * (1.0 - squash))).astype(
        jnp.bfloat16
    )
    grad_up_pre = (grad_hidden * activated).astype(jnp.bfloat16)
    gate_grad = lax.dot_general(
        routed, grad_gate_pre, contract_rows, preferred_element_type=jnp.float32
    ).astype(jnp.bfloat16)[None]
    up_grad = lax.dot_general(
        routed, grad_up_pre, contract_rows, preferred_element_type=jnp.float32
    ).astype(jnp.bfloat16)[None]
    down_grad = lax.dot_general(
        hidden, routed_grad, contract_rows, preferred_element_type=jnp.float32
    ).astype(jnp.bfloat16)[None]
    input_part = lax.dot_general(
        grad_gate_pre, w_gate, contract_cols, preferred_element_type=jnp.float32
    ) + lax.dot_general(grad_up_pre, w_up, contract_cols, preferred_element_type=jnp.float32)
    out_part = out_part.reshape(n_expert, capacity, feat_width)
    input_part = input_part.reshape(n_expert, capacity, feat_width)
    out_share, input_share = (
        lax.psum_scatter(out_part, "tensor", scatter_dimension=2, tiled=True),
        lax.psum_scatter(input_part, "tensor", scatter_dimension=2, tiled=True),
    )
    partial_value = jnp.stack((out_share, input_share))
    kept = jnp.where(parity == 0, partial_value[:, :, :half_cap], partial_value[:, :, half_cap:])
    handed = jnp.where(parity == 0, partial_value[:, :, half_cap:], partial_value[:, :, :half_cap])
    summed = kept + partner(handed, "expert", 0)
    going_back = summed.astype(jnp.bfloat16)
    returned = lax.all_to_all(going_back, "expert", split_axis=1, concat_axis=1, tiled=True)
    home_ids = jnp.arange(n_expert * half_cap, dtype=jnp.int32)
    home_map = (home_ids[:, None] == target_row[None, :]).astype(jnp.bfloat16)
    flat_back = returned.reshape(2, n_expert * half_cap, returned.shape[3])
    gathered_home = jnp.einsum(
        "rt,krw->ktw", home_map, flat_back, preferred_element_type=jnp.float32
    ).astype(jnp.bfloat16)
    return (gathered_home[0], gathered_home[1], gate_grad, up_grad, down_grad)


def expert_kernel(
    tok_hbm, cot_hbm, lab_hbm, dom_hbm, dw_hbm, wg_hbm, wu_hbm, wd_hbm,
    map_hbm, back_hbm, dg_hbm, du_hbm, dd_hbm,
    slot_map, back, dg, du, dd, tok_ref, cot_ref, lab_ref, dom_ref, dw_ref, wg, wu, wd, slots, rows, gate_pre, up_pre, hidden, ggp, gup, keep,
    sib_src, sib_dst, diag_src, diag_dst, nx_src, nx_dst, ny_src, ny_dst,
    back_src, send_sem, recv_sem, local_sem,
):
    n_tok, width = tok_ref.shape
    n_lang = slots.shape[0]
    cap = slots.shape[2]
    half = cap // 2
    block = 2 * cap
    ei = lax.axis_index("expert")
    ti = lax.axis_index("tensor")
    z, y = ei // 2, ei % 2
    x, c = ti // 2, ti % 2
    nx, ny = 1 - x, 1 - y
    tix = nx * 2 + c
    tis = x * 2 + 1 - c
    tixs = nx * 2 + 1 - c
    plane = [z, z + 1 - 2 * (z % 2), (z + 2) % 4, 3 - z]
    x_dev, y_dev, s_dev = (ei, tix), (z * 2 + ny, ti), (ei, tis)
    z_dev = [(plane[j] * 2 + y, ti) for j in range(n_lang)]

    loads = [
        pltpu.make_async_copy(src, dst, local_sem.at[n])
        for n, (src, dst) in enumerate((
            (lab_hbm, lab_ref), (tok_hbm, tok_ref), (dom_hbm, dom_ref), (dw_hbm, dw_ref),
            (cot_hbm, cot_ref), (wg_hbm.at[0], wg), (wu_hbm.at[0], wu), (wd_hbm.at[0], wd),
        ))
    ]
    barrier = pltpu.get_barrier_semaphore()
    others = [x_dev, y_dev, s_dev] + z_dev[1:]
    for dev in others:
        pl.semaphore_signal(barrier, inc=1, device_id=dev, device_id_type=MESH)
    for copy in loads:
        copy.start()

    started = []

    def copy(kind, k, j, src, dst, dev):
        return pltpu.make_async_remote_copy(
            src_ref=src, dst_ref=dst, send_sem=send_sem.at[kind, k, j],
            recv_sem=recv_sem.at[kind, k, j], device_id=dev, device_id_type=MESH,
        )

    def send(kind, k, j, src, dst, dev):
        going = copy(kind, k, j, src, dst, dev)
        going.start()
        started.append(going)

    def recv(kind, k, j, dst, dev):
        copy(kind, k, j, dst, dst, dev).wait_recv()

    def piece(k, f, j, row_y, part=None):
        first = j * block + row_y * cap
        size = cap
        if part is not None:
            first = first + part * half
            size = half
        return rows.at[k, f, pl.ds(pl.multiple_of(first, half), size)]

    loads[0].wait()
    lane = lax.broadcasted_iota(jnp.int32, (n_tok, n_tok), 1)
    sub = lax.broadcasted_iota(jnp.int32, (n_tok, n_tok), 0)

    def column(row_ref):
        wide = jnp.broadcast_to(row_ref[...].astype(F32), (n_tok, n_tok))
        return jnp.sum(jnp.where(lane == sub, wide, 0.0), axis=1, keepdims=True)

    lab = column(lab_ref)
    lab_hot = jnp.where(lane.astype(F32) == lab, 1.0, 0.0)
    earlier = jnp.where(lane < sub, 1.0, 0.0).astype(BF16)
    before = jnp.dot(earlier, lab_hot.astype(BF16), preferred_element_type=F32)
    pos = jnp.sum(before * lab_hot, axis=1, keepdims=True)
    target = lab * cap + pos
    slot_lane = lax.broadcasted_iota(jnp.int32, (n_tok, n_lang * cap), 1).astype(F32)
    to_slot = jnp.where(slot_lane == target, 1.0, 0.0).astype(BF16)
    slot_map[...] = to_slot
    map_store = pltpu.make_async_copy(slot_map, map_hbm, local_sem.at[21])
    map_store.start()
    over_tokens = (((0,), (0,)), ((), ()))

    def pack(k, source):
        packed = lax.dot_general(
            to_slot, source, over_tokens, preferred_element_type=F32
        ).astype(BF16)
        for e in range(n_lang):
            slots[e, k] = packed[e * cap:(e + 1) * cap]

    def exchange(k):
        for j in range(1, n_lang):
            send(ZOUT, k, j, slots.at[plane[j], k], piece(k, ti, j, y), z_dev[j])
        piece(k, ti, 0, y)[...] = slots[z, k]

    loads[1].wait()
    pack(0, tok_ref[...])
    pl.semaphore_wait(barrier, len(others))
    exchange(0)
    for load in loads[2:5]:
        load.wait()
    n_dom = dw_ref.shape[1]
    dom_lane = lax.broadcasted_iota(jnp.int32, (n_tok, n_dom), 1).astype(F32)
    dw_row = jnp.broadcast_to(dw_ref[...], (n_tok, n_dom))
    scale = jnp.sum(
        jnp.where(dom_lane == column(dom_ref), dw_row, 0.0), axis=1, keepdims=True
    )

    order = [(0, 0), (1, 0), (0, 1), (0, 2), (0, 3), (1, 2), (1, 3), (1, 1)]

    def g0(q):
        k, j = order[q]
        own = piece(k, ti, j, y)
        if j:
            recv(ZOUT, k, j, own, z_dev[j])
        send(XOWN, k, j, own, own, x_dev)
        send(YOWN, k, j, own, own, y_dev)
        send(SOWN, k, j, own, own, s_dev)

    def g1(q):
        k, j = order[q]
        from_x, from_y = piece(k, tix, j, y), piece(k, ti, j, ny)
        recv(XOWN, k, j, from_x, x_dev)
        part = piece(k, tix, j, y, 0)
        send(FWDA, k, j, part, part, y_dev)
        send(SPX, k, j, from_x, from_x, s_dev)
        recv(YOWN, k, j, from_y, y_dev)
        part = piece(k, ti, j, ny, 1)
        send(FWDB, k, j, part, part, x_dev)
        send(SPY, k, j, from_y, from_y, s_dev)

    def g2(q):
        k, j = order[q]
        recv(FWDA, k, j, piece(k, tix, j, ny, 0), y_dev)
        recv(FWDB, k, j, piece(k, tix, j, ny, 1), x_dev)
        diag = piece(k, tix, j, ny)
        send(SPD, k, j, diag, diag, s_dev)

    def g3(q):
        k, j = order[q]
        recv(SOWN, k, j, piece(k, tis, j, y), s_dev)
        recv(SPX, k, j, piece(k, tixs, j, y), s_dev)
        recv(SPY, k, j, piece(k, tis, j, ny), s_dev)
        recv(SPD, k, j, piece(k, tixs, j, ny), s_dev)

    size = 2 * block
    n_feat = rows.shape[1]
    over_cols = (((1,), (1,)), ((), ()))

    def all_feats(k, g):
        return jnp.concatenate(
            [rows[k, f, g * size:(g + 1) * size] for f in range(n_feat)], axis=1
        )

    def forward(g):
        at = slice(g * size, (g + 1) * size)
        here = all_feats(0, g)
        gp = jnp.dot(here, wg[...], preferred_element_type=F32)
        up = jnp.dot(here, wu[...], preferred_element_type=F32)
        gate_pre[at] = gp
        up_pre[at] = up
        hidden[at] = (gp * jax.nn.sigmoid(gp) * up).astype(BF16)

    def backward(g):
        at = slice(g * size, (g + 1) * size)
        gh = lax.dot_general(all_feats(1, g), wd[...], over_cols, preferred_element_type=F32)
        gp, up = gate_pre[at], up_pre[at]
        s = jax.nn.sigmoid(gp)
        ggp[at] = (gh * up * s * (1.0 + gp * (1.0 - s))).astype(BF16)
        gup[at] = (gh * (gp * s)).astype(BF16)

    def sums(k, g):
        at = slice(g * size, (g + 1) * size)

        def one(f):
            feats = pl.ds(pl.multiple_of(f * width, width), width)
            if k == 0:
                return jnp.dot(hidden[at], wd[:, feats], preferred_element_type=F32)
            return lax.dot_general(
                ggp[at], wg[feats, :], over_cols, preferred_element_type=F32
            ) + lax.dot_general(gup[at], wu[feats, :], over_cols, preferred_element_type=F32)

        for ax in range(2):
            sib_src[k, ax, at] = one(ax * 2 + 1 - c).astype(BF16)
        for j in (2 * g, 2 * g + 1):
            part = pl.ds(j * block, block)
            send(RSIB, k, j, sib_src.at[k, :, part], sib_dst.at[k, :, part], s_dev)
        for ax in range(2):
            keep[k, ax, at] = one(ax * 2 + c)

    def pair_sum(k, j, at_x, at_y):
        where = pl.ds(pl.multiple_of(j * block + at_y * cap, cap), cap)
        return keep[k, at_x, where] + sib_dst[k, at_x, where].astype(F32)

    def r1(q):
        k, j = q // n_lang, q % n_lang
        part = pl.ds(j * block, block)
        recv(RSIB, k, j, sib_dst.at[k, :, part], s_dev)
        diag_src[k, j] = pair_sum(k, j, nx, ny).astype(BF16)
        top, low = pl.ds(0, half), pl.ds(half, half)
        send(RDA, k, j, diag_src.at[k, j, top], diag_dst.at[k, j, top], y_dev)
        send(RDB, k, j, diag_src.at[k, j, low], diag_dst.at[k, j, low], x_dev)

    def r2(q):
        k, j = q // n_lang, q % n_lang
        top, low = pl.ds(0, half), pl.ds(half, half)
        recv(RDA, k, j, diag_dst.at[k, j, top], y_dev)
        to_x = pair_sum(k, j, nx, y)
        nx_src[k, j, top] = (to_x[:half] + diag_dst[k, j, top].astype(F32)).astype(BF16)
        nx_src[k, j, low] = to_x[half:].astype(BF16)
        send(RX, k, j, nx_src.at[k, j], nx_dst.at[k, j], x_dev)
        recv(RDB, k, j, diag_dst.at[k, j, low], x_dev)
        to_y = pair_sum(k, j, x, ny)
        ny_src[k, j, top] = to_y[:half].astype(BF16)
        ny_src[k, j, low] = (to_y[half:] + diag_dst[k, j, low].astype(F32)).astype(BF16)
        send(RY, k, j, ny_src.at[k, j], ny_dst.at[k, j], y_dev)

    def r3(q):
        k, j = q // n_lang, q % n_lang
        recv(RX, k, j, nx_dst.at[k, j], x_dev)
        recv(RY, k, j, ny_dst.at[k, j], y_dev)
        total = pair_sum(k, j, x, y) + nx_dst[k, j].astype(F32) + ny_dst[k, j].astype(F32)
        if j:
            back_src[k, j] = total.astype(BF16)
            send(RZ, k, j, back_src.at[k, j], back.at[k, z], z_dev[j])
        else:
            back[k, z] = total.astype(BF16)

    over_rows = (((0,), (0,)), ((), ()))

    stores = []

    def store(src, dst):
        going = pltpu.make_async_copy(src, dst, local_sem.at[8 + len(stores)])
        going.start()
        stores.append(going)

    def weight_grad(which, f):
        at = slice(f * width, (f + 1) * width)
        if which == 2:
            dd[0, :, at] = lax.dot_general(
                hidden[...], rows[1, f], over_rows, preferred_element_type=F32
            ).astype(BF16)
            store(dd.at[0, :, at], dd_hbm.at[0, :, at])
        else:
            out, grad, out_hbm = ((dg, ggp, dg_hbm), (du, gup, du_hbm))[which]
            out[0, at] = lax.dot_general(
                rows[0, f], grad[...], over_rows, preferred_element_type=F32
            ).astype(BF16)
            store(out.at[0, at], out_hbm.at[0, at])

    g0(0)
    pack(1, (scale * cot_ref[...].astype(F32)).astype(BF16))
    exchange(1)
    g0(1), g1(0)
    g0(2), g1(1), g2(0)
    g0(3), g1(2), g2(1), g3(0)
    g0(4), g1(3), g2(2), g3(1)
    for load in loads[5:]:
        load.wait()
    g0(5), g1(4), g2(3), g3(2)
    g0(6)
    forward(0)
    g1(5), g2(4), g3(3), g0(7)
    sums(0, 0)
    g1(6), g2(5), g3(4), r1(0)
    forward(1)
    g1(7), g2(6), g3(5), r1(1)
    r2(0), r2(1)
    sums(0, 1)
    g2(7), g3(6), r1(2), r1(3)
    backward(1)
    sums(1, 1)
    g3(7)
    r3(0), r3(1), r2(2), r2(3), r1(6), r1(7)
    backward(0)
    r3(2), r3(3), r2(6), r2(7)
    sums(1, 0)
    r1(5), r1(4), r3(6), r3(7)
    weight_grad(2, 0), weight_grad(2, 1)
    r2(5), r2(4)
    for f in range(2, n_feat):
        weight_grad(2, f)
    weight_grad(0, 0)
    r3(5), r3(4)
    for f in range(1, n_feat):
        weight_grad(0, f)
    for f in range(n_feat):
        weight_grad(1, f)
    for k in range(2):
        for j in range(1, n_lang):
            recv(RZ, k, j, back.at[k, plane[j]], z_dev[j])
    store(back, back_hbm)
    for going in started:
        going.wait_send()
    for going in stores + [map_store]:
        going.wait()


def home_kernel(
    map_hbm, back_hbm, dg_in, du_in, dd_in, y_ref, yg_ref, dg_out, du_out, dd_out,
    slot_map, back, dg, du, dd, sem,
):
    first = [
        pltpu.make_async_copy(map_hbm, slot_map, sem.at[0]),
        pltpu.make_async_copy(back_hbm, back, sem.at[1]),
    ]
    into, outof = [], []
    for src, held, dst in ((dg_in, dg, dg_out), (du_in, du, du_out), (dd_in, dd, dd_out)):
        step = src.shape[1] // 4
        for n in range(4):
            part = pl.ds(n * step, step)
            at = 2 + 2 * len(into)
            into.append(pltpu.make_async_copy(src.at[0, part], held.at[0, part], sem.at[at]))
            outof.append(pltpu.make_async_copy(held.at[0, part], dst.at[0, part], sem.at[at + 1]))
    for going in first + into:
        going.start()
    for going in first:
        going.wait()
    _, n_lang, cap, width = back.shape
    for k, out_ref in enumerate((y_ref, yg_ref)):
        flat = back[k].reshape(n_lang * cap, width)
        out_ref[...] = jnp.dot(slot_map[...], flat, preferred_element_type=F32).astype(BF16)
    for arriving, leaving in zip(into, outof):
        arriving.wait()
        leaving.start()
    for going in outof:
        going.wait()


def fused_body(
    tokens, labels, domain_ids, domain_weights, cotangent, gate_weight, up_weight, down_weight
):
    n_lang = lax.axis_size("expert") // SPLIT
    n_feat = lax.axis_size("tensor")
    n_tok, width = tokens.shape
    cap = 2 * n_tok // n_lang
    n_rows = n_lang * SPLIT * cap
    feats = n_feat * width
    hid = gate_weight.shape[2]
    vmem = pl.BlockSpec(memory_space=pltpu.VMEM)
    hbm = pl.BlockSpec(memory_space=pltpu.HBM)
    out = jax.ShapeDtypeStruct((n_tok, width), BF16)
    slab = pltpu.VMEM((2, n_lang, cap, width), BF16)
    grads = tuple(
        jax.ShapeDtypeStruct(w.shape, BF16) for w in (gate_weight, up_weight, down_weight)
    )
    parts = pl.pallas_call(
        expert_kernel,
        out_shape=(
            jax.ShapeDtypeStruct((n_tok, n_lang * cap), BF16),
            jax.ShapeDtypeStruct((2, n_lang, cap, width), BF16),
        ) + grads,
        in_specs=[hbm] * 8,
        out_specs=(hbm,) * 5,
        scratch_shapes=[
            pltpu.VMEM((n_tok, n_lang * cap), BF16),
            slab,
            pltpu.VMEM(gate_weight.shape, BF16),
            pltpu.VMEM(up_weight.shape, BF16),
            pltpu.VMEM(down_weight.shape, BF16),
            pltpu.VMEM((n_tok, width), BF16),
            pltpu.VMEM((n_tok, width), BF16),
            pltpu.VMEM((1, n_tok), jnp.int32),
            pltpu.VMEM((1, n_tok), jnp.int32),
            pltpu.VMEM((1, domain_weights.shape[0]), F32),
            pltpu.VMEM((feats, hid), BF16),
            pltpu.VMEM((feats, hid), BF16),
            pltpu.VMEM((hid, feats), BF16),
            pltpu.VMEM((n_lang, 2, cap, width), BF16),
            pltpu.VMEM((2, n_feat, n_rows, width), BF16),
            pltpu.VMEM((n_rows, hid), F32),
            pltpu.VMEM((n_rows, hid), F32),
            pltpu.VMEM((n_rows, hid), BF16),
            pltpu.VMEM((n_rows, hid), BF16),
            pltpu.VMEM((n_rows, hid), BF16),
            pltpu.VMEM((2, 2, n_rows, width), F32),
            pltpu.VMEM((2, 2, n_rows, width), BF16),
            pltpu.VMEM((2, 2, n_rows, width), BF16),
            slab, slab, slab, slab, slab, slab, slab,
            pltpu.SemaphoreType.DMA((KINDS, 2, n_lang)),
            pltpu.SemaphoreType.DMA((KINDS, 2, n_lang)),
            pltpu.SemaphoreType.DMA((22,)),
        ],
        compiler_params=pltpu.CompilerParams(
            collective_id=0, has_side_effects=True, vmem_limit_bytes=58 * 2**20
        ),
        name="expert_layer",
    )(
        tokens, cotangent, labels.reshape(1, n_tok), domain_ids.reshape(1, n_tok),
        domain_weights.reshape(1, -1), gate_weight, up_weight, down_weight,
    )
    return pl.pallas_call(
        home_kernel,
        out_shape=(out, out) + grads,
        in_specs=[hbm] * 5,
        out_specs=(vmem, vmem, hbm, hbm, hbm),
        scratch_shapes=[
            pltpu.VMEM((n_tok, n_lang * cap), BF16),
            slab,
            pltpu.VMEM(gate_weight.shape, BF16),
            pltpu.VMEM(up_weight.shape, BF16),
            pltpu.VMEM(down_weight.shape, BF16),
            pltpu.SemaphoreType.DMA((26,)),
        ],
        compiler_params=pltpu.CompilerParams(vmem_limit_bytes=58 * 2**20),
        name="home",
    )(*parts)


def solution(mesh):
    n_lang = mesh.shape["expert"] // SPLIT
    fits = n_lang == 4 and mesh.shape["tensor"] == 4
    return jax.shard_map(
        fused_body if fits else body,
        mesh=mesh,
        in_specs=(
            P("expert", "tensor"),
            P("expert", None),
            P("expert"),
            P(),
            P("expert", "tensor"),
            P("expert", None, "tensor"),
            P("expert", None, "tensor"),
            P("expert", "tensor", None),
        ),
        out_specs=(
            P("expert", "tensor"),
            P("expert", "tensor"),
            P("expert", None, "tensor"),
            P("expert", None, "tensor"),
            P("expert", "tensor", None),
        ),
        check_vma=False,
    )
```
